32 devices in a mesh: rep: 2 (over x), gx: 16 (over z, y, core).
Axes of the slice: x: 2, y: 2, z: 4, core: 2. Of those that a mesh axis runs over, the one named last changes fastest.
Arguments:
- first_tokens: bfloat16 [64, 18432], P('rep', 'gx'), parts along dimension 0, may hold values from -6 to 6
- second_tokens: bfloat16 [64, 18432], P('rep', 'gx'), parts along dimension 0, may hold values from -6 to 6
- ln_gain: bfloat16 [18432], P('gx'), may hold values from 0.099609375 to 1.8984375
- qkv_weight: bfloat16 [18432, 6656], P('gx')
- out_weight: bfloat16 [6144, 18432], P(None, 'gx'), may hold values from -0.078125 to 0.078125
- kv_cache: bfloat16 [64, 1024, 512], P(('rep', 'gx')), parts along dimension 0, as said below
- lengths: int32 [64], P(('rep', 'gx')), parts along dimension 0, may hold values from 256 to 1024, as said below
- order: int32 [64], P('rep'), parts along dimension 0, may hold values from 0 to 31, each once
Outputs:
- first_out: bfloat16 [64, 18432], P('rep', 'gx'), parts along dimension 0
- second_out: bfloat16 [64, 18432], P('rep', 'gx'), parts along dimension 0
The draws below stay inside these ranges and needn't reach their ends.
There are 2 independent parts, one for each index of `rep`. The reference program is written for one: setup_inputs(seed, part) draws one part's arguments, and reference() takes and returns one part's arrays. A program takes and returns all parts, laid end to end along the dimension named above; an argument that names none is the same for every part. Nothing has to cross between parts.
Inputs may be any that keep to these rules, and one draw needn't show every extreme that they name: `lengths`: some slot has exactly 256 and some slot exactly 1024 cached positions. `kv_cache`: entries of key columns and value columns are finite; a request's key scale may differ from another's.
All inputs are finite; a program needn't handle non-finite values.
Results may differ from the reference program's by a relative error of at most 0.005.
The reference program's roundings to bfloat16 on the way count: a program that leaves them out, or rounds other values in their place, can miss the bound.
Values may be sent and summed in bfloat16 or wider, within the bound.
A program may use at most 128 MiB of HBM per device.

```python
import math
import jax
import jax.numpy as jnp
from jax import lax

D = 18432
HEADS = 24
HD = 256
CTX = 1024
REQUESTS = 32
QKV = 6656


def draw_qkv_weight(key, part):
    key = jax.random.fold_in(key, 11)
    normal_draw = jax.random.normal(key, (D, QKV), jnp.float32)
    column = jnp.arange(QKV)
    factor = jnp.where(column < HEADS * HD, 3.0, 1.0) / math.sqrt(D)
    return (normal_draw * factor[None, :]).astype(jnp.bfloat16)


def draw_kv_cache(key, part):
    key = jax.random.fold_in(key, 12)
    first_key = jax.random.fold_in(key, 0)
    return jax.random.normal(first_key, (REQUESTS, CTX, 2 * HD), jnp.float32).astype(jnp.bfloat16)


def draw_lengths(key, part):
    key = jax.random.fold_in(key, 13)
    first_key, second_key, third_key = jax.random.split(key, 3)
    values = jax.random.randint(first_key, (REQUESTS,), CTX // 4, CTX + 1)
    longest = jax.random.randint(second_key, (), 0, REQUESTS)
    shortest = (longest + 1 + jax.random.randint(third_key, (), 0, REQUESTS - 1)) % REQUESTS
    slots = jnp.arange(REQUESTS)
    values = jnp.where(slots == longest, CTX, values)
    values = jnp.where(slots == shortest, CTX // 4, values)
    return values.astype(jnp.int32)


def steps_of(own_key, dims, shards, low, top_value):
    level = 1.0
    for axis_at, parts in shards:
        heights = jax.random.uniform(jax.random.fold_in(jax.random.fold_in(own_key, 6), axis_at), (parts,), jnp.float32, low / len(shards), top_value / len(shards))
        level = level * jnp.repeat(jnp.exp(heights), dims[axis_at] // parts).reshape((-1,) + (1,) * (len(dims) - 1 - axis_at))
    return level


def scatter_about(key, shape, scale, reach, shards=(), kind=jnp.bfloat16):
    array = jax.random.normal(key, shape, jnp.float32) * scale
    if len(shards) > 0:
        array = steps_of(key, shape, shards, -0.22, 0.18) * array
    return jnp.clip(array, min=-reach, max=reach).astype(kind)


def setup_inputs(seed: int = 0, part: int = 0) -> dict:
    splits = jax.random.split(jax.random.key(seed), 9)
    own_keys = jax.random.split(jax.random.fold_in(splits[8], part), 9)
    return {
        "first_tokens": scatter_about(own_keys[0], (REQUESTS, D), 1.0, 6.0, ((1, 16),)),
        "second_tokens": scatter_about(own_keys[1], (REQUESTS, D), 1.0, 6.0, ((1, 16),)),
        "ln_gain": jnp.clip(1.0 + 0.18 * jax.random.normal(splits[2], (D,), jnp.float32), 0.099609375, 1.8984375).astype(jnp.bfloat16),
        "qkv_weight": draw_qkv_weight(jax.random.fold_in(splits[8], 71), part),
        "out_weight": scatter_about(splits[4], (HEADS * HD, D), (HEADS * HD) ** -0.5, 0.078125, ((1, 16),)),
        "kv_cache": draw_kv_cache(jax.random.fold_in(jax.random.fold_in(splits[8], part), 71), part),
        "lengths": draw_lengths(jax.random.fold_in(jax.random.fold_in(splits[8], part), 71), part),
        "order": jax.random.permutation(own_keys[7], REQUESTS).astype(jnp.int32),
    }


eps_norm = 1e-05

def rotate(vectors, positions):
    half_width = vectors.shape[-1] // 2
    frequencies = 10000.0 ** (-jnp.arange(half_width, dtype=jnp.float32) / half_width)
    angles = positions.astype(jnp.float32)[..., None] * frequencies
    cosines = jnp.cos(angles)
    sine_terms = jnp.sin(angles)
    lower_half = vectors[..., :half_width]
    upper_half = vectors[..., half_width:]
    return jnp.concatenate([lower_half * cosines - upper_half * sine_terms, upper_half * cosines + lower_half * sine_terms], axis=-1)

def normalize(token_rows, gain):
    widened = token_rows.astype(jnp.float32)
    totals = lax.optimization_barrier(jnp.sum(widened, axis=1))
    squares = lax.optimization_barrier(jnp.sum(widened * widened, axis=1))
    mean_value = totals / D
    variance = squares / D - mean_value * mean_value
    scaled = (widened - mean_value[:, None]) * lax.rsqrt(variance[:, None] + eps_norm)
    return (scaled * gain.astype(jnp.float32)).astype(jnp.bfloat16)

def split_heads(projected, positions):
    queries = projected[:, :HEADS * HD].reshape(projected.shape[0], HEADS, HD)
    queries = rotate(queries, positions[:, None]).astype(jnp.bfloat16)
    keys_new = rotate(projected[:, HEADS * HD:HEADS * HD + HD], positions).astype(jnp.bfloat16)
    values_new = projected[:, HEADS * HD + HD:].astype(jnp.bfloat16)
    return (queries, keys_new, values_new)

def attend(slot_data):
    queries, cache_block, length, keys_new, values_new = slot_data
    score_scale = HD ** (-0.5)
    high = lax.Precision.HIGHEST
    query_wide = queries.astype(jnp.float32)
    cached_keys = cache_block[:, :HD].astype(jnp.float32)
    cached_values = cache_block[:, HD:].astype(jnp.float32)
    scores_old = jnp.dot(query_wide, cached_keys.T, precision=high) * score_scale
    live_mask = jnp.arange(cache_block.shape[0]) < length
    scores_old = jnp.where(live_mask[None, :], scores_old, -jnp.inf)
    scores_new = jnp.dot(query_wide, keys_new.astype(jnp.float32).T, precision=high) * score_scale
    peak_score = jnp.maximum(lax.optimization_barrier(jnp.max(scores_old, axis=1)), lax.optimization_barrier(jnp.max(scores_new, axis=1)))
    weights_old = jnp.exp(scores_old - peak_score[:, None])
    weights_new = jnp.exp(scores_new - peak_score[:, None])
    denominator = lax.optimization_barrier(jnp.sum(weights_old, axis=1)) + lax.optimization_barrier(jnp.sum(weights_new, axis=1))
    rounded_old = lax.optimization_barrier(weights_old.astype(jnp.bfloat16)).astype(jnp.float32)
    rounded_new = lax.optimization_barrier(weights_new.astype(jnp.bfloat16)).astype(jnp.float32)
    weighted = jnp.dot(rounded_old, cached_values, precision=high)
    weighted = weighted + jnp.dot(rounded_new, values_new.astype(jnp.float32), precision=high)
    return (weighted / denominator[:, None]).astype(jnp.bfloat16)

def reference(first_tokens, second_tokens, ln_gain, qkv_weight, out_weight, kv_cache, lengths, order):
    request_count = order.shape[0]
    inverse = jnp.zeros((request_count,), jnp.int32).at[order].set(jnp.arange(request_count, dtype=jnp.int32))
    projections = []
    for token_rows, offset in ((first_tokens, 0), (second_tokens, 1)):
        slot_rows = normalize(token_rows, ln_gain)[order]
        projected = jnp.dot(slot_rows, qkv_weight, preferred_element_type=jnp.float32)
        projections.append(split_heads(projected, lengths + offset))
    first_q, first_k, first_v = projections[0]
    second_q, second_k, second_v = projections[1]
    pairs = ((first_q, first_k[:, None], first_v[:, None]), (second_q, jnp.stack([first_k, second_k], 1), jnp.stack([first_v, second_v], 1)))
    results = []
    for queries, keys_new, values_new in pairs:
        heads = lax.map(attend, (queries, kv_cache, lengths, keys_new, values_new))
        mixed = jnp.dot(heads.reshape(request_count, HEADS * HD), out_weight, preferred_element_type=jnp.float32)
        results.append(mixed[inverse])
    first_out = (first_tokens.astype(jnp.float32) + results[0]).astype(jnp.bfloat16)
    second_out = (second_tokens.astype(jnp.float32) + results[1]).astype(jnp.bfloat16)
    return (first_out, second_out)
```

```python
import functools

import jax
import jax.numpy as jnp
import numpy as np
from jax import lax
from jax.experimental import pallas as pl
from jax.experimental.pallas import tpu as pltpu
from jax.sharding import PartitionSpec as P

D = 18432
HEADS = 24
HD = 256
HALF = HD // 2
KV = 2 * HD

GROUP = 8
GROUPS = HEADS // GROUP
TILE = 512

eps_norm = 1e-05

F32 = jnp.float32
BF16 = jnp.bfloat16


def dot_nt(a, b):
    return lax.dot_general(a, b, (((1,), (1,)), ((), ())), preferred_element_type=F32)


def dot_nn(a, b):
    return jnp.dot(a, b, preferred_element_type=F32)


def chunk_columns(j):
    width = GROUP * HD
    return (0, KV + width) if j == 0 else (KV + j * width, width)


def kernel(
    n,
    slots,
    first_ref,
    second_ref,
    gain_ref,
    freq_ref,
    qkv_ref,
    out_w_ref,
    cache_ref,
    lengths_ref,
    order_ref,
    first_out_ref,
    second_out_ref,
    x,
    wq,
    wo,
    cache,
    stat_own,
    stat_in,
    normed,
    partial,
    from_core,
    from_mid,
    from_hi,
    query,
    new_kv,
    gathered,
    spread,
    lhs,
    total,
    in_sem,
    q_sem,
    o_sem,
    stat_send,
    stat_recv,
    core_send,
    core_recv,
    mid_send,
    mid_recv,
    hi_send,
    hi_recv,
    ghi_send,
    ghi_recv,
    gmid_send,
    gmid_recv,
    gcore_send,
    gcore_recv,
):
    H = n // 4
    R = order_ref.shape[0]
    N = 2 * R
    rp = 2 * slots
    me = lax.axis_index("gx")
    core, mid, hi = me % 2, (me // 2) % 2, me // 4

    def index_of(hi_at, mid_at, core_at):
        return (hi_at * 2 + mid_at) * 2 + core_at

    sibling = index_of(hi, mid, 1 - core)
    across = index_of(hi, 1 - mid, core)
    ahead = [lax.rem(hi + d, H) for d in range(H)]
    behind = [lax.rem(hi - d + H, H) for d in range(H)]

    loads = [
        pltpu.make_async_copy(first_ref, x.at[pl.ds(0, R)], in_sem.at[0]),
        pltpu.make_async_copy(second_ref, x.at[pl.ds(R, R)], in_sem.at[1]),
    ]
    width = GROUP * HD
    kv_load = pltpu.make_async_copy(
        qkv_ref.at[:, pl.ds(HEADS * HD, KV)], wq.at[:, pl.ds(0, KV)], q_sem.at[GROUPS]
    )
    q_loads = [
        pltpu.make_async_copy(
            qkv_ref.at[:, pl.ds(j * width, width)],
            wq.at[:, pl.ds(KV + j * width, width)],
            q_sem.at[j],
        )
        for j in range(GROUPS)
    ]
    cache_load = pltpu.make_async_copy(cache_ref, cache, in_sem.at[2])
    o_loads = [
        pltpu.make_async_copy(
            out_w_ref.at[pl.ds(j * width, width)], wo.at[pl.ds(j * width, width)], o_sem.at[j]
        )
        for j in range(GROUPS)
    ]
    for copy in loads + [kv_load] + q_loads + [cache_load] + o_loads:
        copy.start()

    barrier = pltpu.get_barrier_semaphore()
    partners = [sibling, across] + [index_of(ahead[d], mid, core) for d in range(1, H)]
    for partner in partners:
        pl.semaphore_signal(
            barrier, inc=1, device_id={"gx": partner}, device_id_type=pl.DeviceIdType.MESH
        )

    sent = []

    def send(src, dst, send_sem, recv_sem, partner):
        copy = pltpu.make_async_remote_copy(
            src_ref=src,
            dst_ref=dst,
            send_sem=send_sem,
            recv_sem=recv_sem,
            device_id={"gx": partner},
            device_id_type=pl.DeviceIdType.MESH,
        )
        copy.start()
        sent.append(copy)
        return copy

    for copy in loads:
        copy.wait()
    rows = x[...]
    features = rows.shape[1]
    square = lax.broadcasted_iota(jnp.int32, (N, N), 0)
    across_lanes = lax.broadcasted_iota(jnp.int32, (N, N), 1)
    diagonal = square == across_lanes
    sums = dot_nt(jnp.ones((8, features), BF16), rows)
    squares = jnp.sum(jnp.where(diagonal, dot_nt(rows, rows), 0.0), axis=0, keepdims=True)
    line = lax.broadcasted_iota(jnp.int32, (8, N), 0)
    stat_own[...] = jnp.zeros_like(stat_own)
    stat_own[0, :, :N] = jnp.where(line == 0, sums, jnp.broadcast_to(squares, (8, N)))

    pl.semaphore_wait(barrier, len(partners))

    copy = send(stat_own.at[0], stat_in.at[0], stat_send.at[0], stat_recv.at[0], sibling)

    lane = lax.broadcasted_iota(jnp.int32, (8, N), 1)
    holder = jnp.zeros((8, N), jnp.int32)
    for p in range(R):
        device, slot = p // slots, p % slots
        at = (((device % 2) * 2 + (device // 2) % 2) * H + device // 4) * slots + slot
        holder = jnp.where(lane // 2 == at, order_ref[p], holder)
    holder = holder + (lane % 2) * R
    to_request = jnp.where(square == jnp.broadcast_to(holder[:1], (N, N)), 1.0, 0.0).astype(BF16)
    unit = jnp.where(diagonal, 1.0, 0.0).astype(BF16)
    to_slot = dot_nt(unit, to_request).astype(BF16)

    def rotation(count, per_row):
        row = lax.broadcasted_iota(jnp.int32, (count, HALF), 0)
        position = jnp.zeros((count, HALF), jnp.int32)
        for slot in range(slots):
            position = jnp.where(row // (2 * per_row) == slot, lengths_ref[slot], position)
        position = position + (row // per_row) % 2
        angles = position.astype(F32) * freq_ref[...]
        return jnp.cos(angles), jnp.sin(angles)

    q_cos, q_sin = rotation(rp * GROUP, GROUP)

    copy.wait_recv()
    stat_own[1] = stat_own[0] + stat_in[0]
    copy = send(stat_own.at[1], stat_in.at[1], stat_send.at[1], stat_recv.at[1], across)
    k_cos, k_sin = rotation(rp, 1)
    copy.wait_recv()
    stat_own[2] = stat_own[1] + stat_in[1]
    copies = [
        send(
            stat_own.at[2],
            stat_in.at[1 + d],
            stat_send.at[1 + d],
            stat_recv.at[1 + d],
            index_of(ahead[d], mid, core),
        )
        for d in range(1, H)
    ]
    for copy in copies:
        copy.wait_recv()
    stats = stat_own[2]
    for d in range(1, H):
        stats = stats + stat_in[1 + d]

    def as_column(row):
        return jnp.sum(
            jnp.where(diagonal, jnp.broadcast_to(row, (N, N)), 0.0), axis=1, keepdims=True
        )

    mean = as_column(stats[0:1, :N]) / D
    variance = as_column(stats[1:2, :N]) / D - mean * mean
    scaled = (rows.astype(F32) - mean) * lax.rsqrt(variance + eps_norm)
    by_request = (scaled * gain_ref[...].astype(F32)).astype(BF16)
    normed[...] = dot_nn(to_slot, by_request).astype(BF16)

    def project(j):
        start, count = chunk_columns(j)
        if j == 0:
            kv_load.wait()
        q_loads[j].wait()

        @pl.loop(0, count // TILE)
        def _(i):
            at = pl.ds(pl.multiple_of(start + i * TILE, TILE), TILE)
            product = dot_nn(normed[...], wq[:, at])
            for g in range(n):
                partial[g // (2 * H), (g // H) % 2, g % H, :, at] = product[
                    g * rp : (g + 1) * rp
                ]

        at = pl.ds(start, count)
        return send(
            partial.at[1 - core, :, :, :, at],
            from_core.at[:, :, :, at],
            core_send.at[j],
            core_recv.at[j],
            sibling,
        )

    def add_core(j, copy):
        start, count = chunk_columns(j)
        at = pl.ds(start, count)
        copy.wait_recv()
        from_core[1 - mid, :, :, at] = from_core[1 - mid, :, :, at] + partial[core, 1 - mid, :, :, at]
        copy = send(
            from_core.at[1 - mid, :, :, at],
            from_mid.at[:, :, at],
            mid_send.at[j],
            mid_recv.at[j],
            across,
        )
        from_core[mid, :, :, at] = from_core[mid, :, :, at] + partial[core, mid, :, :, at]
        return copy

    def add_mid(j, copy):
        start, count = chunk_columns(j)
        at = pl.ds(start, count)
        copy.wait_recv()
        from_mid[:, :, at] = from_mid[:, :, at] + from_core[mid, :, :, at]
        return [
            send(
                from_mid.at[ahead[d], :, at],
                from_hi.at[d - 1, :, at],
                hi_send.at[j, d - 1],
                hi_recv.at[j, d - 1],
                index_of(ahead[d], mid, core),
            )
            for d in range(1, H)
        ]

    def turn(lower, upper, cosines, sines):
        return jnp.concatenate(
            [lower * cosines - upper * sines, upper * cosines + lower * sines], axis=1
        )

    def attend(j, copies):
        start, count = chunk_columns(j)
        at = pl.ds(start, count)
        for copy in copies:
            copy.wait_recv()
        rows = from_mid[hi, :, at]
        for d in range(1, H):
            rows = rows + from_hi[d - 1, :, at]
        q_start = 0
        if j == 0:
            q_start = KV
            keys = turn(rows[:, :HALF], rows[:, HALF:HD], k_cos, k_sin)
            both = jnp.concatenate([keys, rows[:, HD:KV]], axis=1)
            at_row = lax.broadcasted_iota(jnp.int32, (128, KV), 0)
            for slot in range(slots):
                one = jnp.broadcast_to(both[2 * slot : 2 * slot + 1], (128, KV))
                two = jnp.broadcast_to(both[2 * slot + 1 : 2 * slot + 2], (128, KV))
                padded = jnp.where(at_row == 0, one, jnp.where(at_row == 1, two, 0.0))
                new_kv[slot] = padded.astype(BF16)
            cache_load.wait()
        for h in range(GROUP):
            for part in range(2):
                begin = q_start + h * HD + part * HALF
                query[part, pl.ds(h, rp, stride=GROUP), :] = rows[:, begin : begin + HALF]
        queries = turn(query[0], query[1], q_cos, q_sin)
        scale = HD ** (-0.5)
        context = cache.shape[1]
        span = 2 * GROUP
        lane_old = lax.broadcasted_iota(jnp.int32, (span, context), 1)
        lane_new = lax.broadcasted_iota(jnp.int32, (span, 128), 1)
        step = lax.broadcasted_iota(jnp.int32, (span, 128), 0) // GROUP
        results = []
        for slot in range(slots):
            q = queries[slot * span : (slot + 1) * span].astype(BF16)
            old = dot_nt(q, cache[slot, :, :HD]) * scale
            new = dot_nt(q, new_kv[slot, :, :HD]) * scale
            old = jnp.where(lane_old < lengths_ref[slot], old, -jnp.inf)
            new = jnp.where(lane_new <= step, new, -jnp.inf)
            peak = jnp.maximum(
                jnp.max(old, axis=1, keepdims=True), jnp.max(new, axis=1, keepdims=True)
            )
            old = jnp.exp(old - peak)
            new = jnp.exp(new - peak)
            denominator = jnp.sum(old, axis=1, keepdims=True) + jnp.sum(
                new, axis=1, keepdims=True
            )
            weighted = dot_nn(old.astype(BF16), cache[slot, :, HD:])
            weighted = weighted + dot_nn(new.astype(BF16), new_kv[slot, :, HD:])
            results.append(weighted / denominator)
        gathered[j, core, mid, hi] = jnp.concatenate(results, axis=0).astype(BF16)
        block = gathered.at[j, core, mid, hi]
        return [
            send(
                block,
                block,
                ghi_send.at[j, d - 1],
                ghi_recv.at[j, d - 1],
                index_of(ahead[d], mid, core),
            )
            for d in range(1, H)
        ]

    def pass_mid(j, copies):
        for copy in copies:
            copy.wait_recv()
        block = gathered.at[j, core, mid]
        return send(block, block, gmid_send.at[j], gmid_recv.at[j], across)

    def pass_core(j, copy):
        copy.wait_recv()
        block = gathered.at[j, core]
        return send(block, block, gcore_send.at[j], gcore_recv.at[j], sibling)

    def mix(j, copy):
        copy.wait_recv()
        o_loads[j].wait()
        everything = gathered[j].reshape(N * GROUP, HD).astype(F32)
        spread[0] = everything[:, :HALF]
        spread[1] = everything[:, HALF:]
        for h in range(GROUP):
            head = jnp.concatenate(
                [spread[part, pl.ds(h, N, stride=GROUP), :] for part in range(2)], axis=1
            ).astype(BF16)
            lhs[:, h * HD : (h + 1) * HD] = dot_nn(to_request, head).astype(BF16)

        for k in range(0, width, 512):
            product = dot_nn(lhs[:, k : k + 512], wo[j * width + k : j * width + k + 512, :])
            if j == 0 and k == 0:
                total[...] = product
            else:
                total[...] += product

    a0 = project(0)
    a1 = project(1)
    b0 = add_core(0, a0)
    a2 = project(2)
    b1 = add_core(1, a1)
    b2 = add_core(2, a2)
    c0 = add_mid(0, b0)
    c1 = add_mid(1, b1)
    g0 = attend(0, c0)
    c2 = add_mid(2, b2)
    g1 = attend(1, c1)
    g0 = pass_mid(0, g0)
    g2 = attend(2, c2)
    g1 = pass_mid(1, g1)
    g0 = pass_core(0, g0)
    g2 = pass_mid(2, g2)
    g1 = pass_core(1, g1)
    mix(0, g0)
    g2 = pass_core(2, g2)
    mix(1, g1)
    mix(2, g2)
    first_out_ref[...] = (x[:R].astype(F32) + total[:R]).astype(BF16)
    second_out_ref[...] = (x[R:].astype(F32) + total[R:]).astype(BF16)
    for copy in sent:
        copy.wait_send()


def on_device(
    n, first_tokens, second_tokens, ln_gain, qkv_weight, out_weight, kv_cache, lengths, order
):
    R, features = first_tokens.shape
    slots, context, _ = kv_cache.shape
    N, rp, H = 2 * R, 2 * slots, n // 4
    columns = qkv_weight.shape[1]
    lanes = max(N, 128)
    frequencies = (10000.0 ** (-np.arange(HALF) / HALF)).astype(np.float32)[None]
    anywhere = pl.BlockSpec(memory_space=pl.ANY)
    vmem = pl.BlockSpec(memory_space=pltpu.VMEM)
    smem = pl.BlockSpec(memory_space=pltpu.SMEM)
    dma = pltpu.SemaphoreType.DMA
    return pl.pallas_call(
        functools.partial(kernel, n, slots),
        out_shape=[jax.ShapeDtypeStruct((R, features), BF16)] * 2,
        in_specs=[anywhere, anywhere, vmem, vmem, anywhere, anywhere, anywhere, smem, smem],
        out_specs=[vmem, vmem],
        scratch_shapes=[
            pltpu.VMEM((N, features), BF16),
            pltpu.VMEM((features, columns), BF16),
            pltpu.VMEM((HEADS * HD, features), BF16),
            pltpu.VMEM((slots, context, KV), BF16),
            pltpu.VMEM((3, 8, lanes), F32),
            pltpu.VMEM((H + 1, 8, lanes), F32),
            pltpu.VMEM((N, features), BF16),
            pltpu.VMEM((2, 2, H, rp, columns), F32),
            pltpu.VMEM((2, H, rp, columns), F32),
            pltpu.VMEM((H, rp, columns), F32),
            pltpu.VMEM((H - 1, rp, columns), F32),
            pltpu.VMEM((2, rp * GROUP, HALF), F32),
            pltpu.VMEM((slots, 128, KV), BF16),
            pltpu.VMEM((GROUPS, 2, 2, H, rp * GROUP, HD), BF16),
            pltpu.VMEM((2, N * GROUP, HALF), F32),
            pltpu.VMEM((N, GROUP * HD), BF16),
            pltpu.VMEM((N, features), F32),
            dma((3,)),
            dma((GROUPS + 1,)),
            dma((GROUPS,)),
            dma((H + 1,)),
            dma((H + 1,)),
            dma((GROUPS,)),
            dma((GROUPS,)),
            dma((GROUPS,)),
            dma((GROUPS,)),
            dma((GROUPS, H - 1)),
            dma((GROUPS, H - 1)),
            dma((GROUPS, H - 1)),
            dma((GROUPS, H - 1)),
            dma((GROUPS,)),
            dma((GROUPS,)),
            dma((GROUPS,)),
            dma((GROUPS,)),
        ],
        compiler_params=pltpu.CompilerParams(
            collective_id=0, has_side_effects=True, vmem_limit_bytes=56 * 2**20
        ),
    )(
        first_tokens,
        second_tokens,
        ln_gain[None],
        jnp.asarray(frequencies),
        qkv_weight,
        out_weight,
        kv_cache,
        lengths,
        order,
    )


def solution(mesh):
    return jax.shard_map(
        functools.partial(on_device, mesh.shape["gx"]),
        mesh=mesh,
        in_specs=(
            P("rep", "gx"),
            P("rep", "gx"),
            P("gx"),
            P("gx", None),
            P(None, "gx"),
            P(("rep", "gx"), None, None),
            P(("rep", "gx")),
            P("rep"),
        ),
        out_specs=(P("rep", "gx"), P("rep", "gx")),
        check_vma=False,
    )
```

```python
import functools

import jax
import jax.numpy as jnp
import numpy as np
from jax import lax
from jax.experimental import pallas as pl
from jax.experimental.pallas import tpu as pltpu
from jax.sharding import PartitionSpec as P

D = 18432
HEADS = 24
HD = 256
HALF = HD // 2
KV = 2 * HD

SIZES = (8, 8, 8)
STARTS = (0, 8, 16)
GROUPS = len(SIZES)
TILE = 512
LOADS_A_STEP = 1

SCHEDULE = (
    (0, 0), (0, 1), (1, 0), (0, 2), (1, 1), (1, 2), (2, 0), (2, 1), (3, 0), (2, 2),
    (3, 1), (4, 0), (3, 2), (4, 1), (5, 0), (4, 2), (5, 1), (6, 0), (5, 2), (6, 1), (6, 2),
)

eps_norm = 1e-05

F32 = jnp.float32
BF16 = jnp.bfloat16


def dot_nt(a, b):
    return lax.dot_general(a, b, (((1,), (1,)), ((), ())), preferred_element_type=F32)


def dot_nn(a, b):
    return jnp.dot(a, b, preferred_element_type=F32)


def chunk_columns(j):
    width = SIZES[j] * HD
    return (0, KV + width) if j == 0 else (KV + STARTS[j] * HD, width)


def kernel(
    n,
    slots,
    first_ref,
    second_ref,
    gain_ref,
    freq_ref,
    qkv_ref,
    out_w_ref,
    cache_ref,
    lengths_ref,
    order_ref,
    total,
    x,
    gain,
    freq,
    lengths,
    order,
    wq,
    wo,
    cache,
    stat_own,
    stat_in,
    normed,
    partial,
    from_core,
    from_mid,
    from_hi,
    query,
    new_kv,
    gathered,
    spread,
    lhs,
    in_sem,
    q_sem,
    o_sem,
    stat_send,
    stat_recv,
    core_send,
    core_recv,
    mid_send,
    mid_recv,
    hi_send,
    hi_recv,
    ghi_send,
    ghi_recv,
    gmid_send,
    gmid_recv,
    gcore_send,
    gcore_recv,
):
    H = n // 4
    R = order_ref.shape[0]
    N = 2 * R
    rp = 2 * slots
    me = lax.axis_index("gx")
    core, mid, hi = me % 2, (me // 2) % 2, me // 4

    def index_of(hi_at, mid_at, core_at):
        return (hi_at * 2 + mid_at) * 2 + core_at

    sibling = index_of(hi, mid, 1 - core)
    across = index_of(hi, 1 - mid, core)
    ahead = [lax.rem(hi + d, H) for d in range(H)]
    behind = [lax.rem(hi - d + H, H) for d in range(H)]

    barrier = pltpu.get_barrier_semaphore()
    partners = [lax.rem(me + d, n) for d in range(1, n)]
    for partner in partners:
        pl.semaphore_signal(
            barrier, inc=1, device_id={"gx": partner}, device_id_type=pl.DeviceIdType.MESH
        )

    loads = [
        pltpu.make_async_copy(src, dst, in_sem.at[i])
        for i, (src, dst) in enumerate(
            [
                (first_ref, x.at[pl.ds(0, R)]),
                (second_ref, x.at[pl.ds(R, R)]),
                (gain_ref, gain),
                (freq_ref, freq),
                (lengths_ref, lengths),
                (order_ref, order),
            ]
        )
    ]
    kv_load = pltpu.make_async_copy(
        qkv_ref.at[:, pl.ds(HEADS * HD, KV)], wq.at[:, pl.ds(0, KV)], q_sem.at[GROUPS]
    )
    q_loads = [
        pltpu.make_async_copy(
            qkv_ref.at[:, pl.ds(start * HD, size * HD)],
            wq.at[:, pl.ds(KV + start * HD, size * HD)],
            q_sem.at[j],
        )
        for j, (start, size) in enumerate(zip(STARTS, SIZES))
    ]
    cache_load = pltpu.make_async_copy(cache_ref, cache, in_sem.at[6])
    o_loads = [
        pltpu.make_async_copy(
            out_w_ref.at[pl.ds(start * HD, size * HD)],
            wo.at[pl.ds(start * HD, size * HD)],
            o_sem.at[j],
        )
        for j, (start, size) in enumerate(zip(STARTS, SIZES))
    ]
    for copy in loads + [kv_load, q_loads[0]]:
        copy.start()

    sent = []

    def send(src, dst, send_sem, recv_sem, partner):
        copy = pltpu.make_async_remote_copy(
            src_ref=src,
            dst_ref=dst,
            send_sem=send_sem,
            recv_sem=recv_sem,
            device_id={"gx": partner},
            device_id_type=pl.DeviceIdType.MESH,
        )
        copy.start()
        sent.append(copy)
        return copy

    for copy in loads:
        copy.wait()
    rows = x[...]
    features = rows.shape[1]
    square = lax.broadcasted_iota(jnp.int32, (N, N), 0)
    across_lanes = lax.broadcasted_iota(jnp.int32, (N, N), 1)
    diagonal = square == across_lanes
    sums = dot_nt(jnp.ones((8, features), BF16), rows)
    squares = jnp.sum(jnp.where(diagonal, dot_nt(rows, rows), 0.0), axis=0, keepdims=True)
    line = lax.broadcasted_iota(jnp.int32, (8, N), 0)
    stat_own[...] = jnp.where(line == 0, sums, jnp.broadcast_to(squares, (8, N)))[:2]

    pl.semaphore_wait(barrier, n - 1)
    copies = [
        send(stat_own, stat_in.at[d - 1], stat_send.at[d - 1], stat_recv.at[d - 1], partners[d - 1])
        for d in range(1, n)
    ]
    for copy in [q_loads[1]]:
        copy.start()

    lane = lax.broadcasted_iota(jnp.int32, (8, N), 1)
    holder = jnp.zeros((8, N), jnp.int32)
    for p in range(R):
        device, slot = p // slots, p % slots
        at = (((device % 2) * 2 + (device // 2) % 2) * H + device // 4) * slots + slot
        holder = jnp.where(lane // 2 == at, order[p], holder)
    holder = holder + (lane % 2) * R
    to_request = jnp.where(square == jnp.broadcast_to(holder[:1], (N, N)), 1.0, 0.0).astype(BF16)
    unit = jnp.where(diagonal, 1.0, 0.0).astype(BF16)
    to_slot = dot_nt(unit, to_request).astype(BF16)

    def rotation(count, per_row):
        row = lax.broadcasted_iota(jnp.int32, (count, HALF), 0)
        position = jnp.zeros((count, HALF), jnp.int32)
        for slot in range(slots):
            position = jnp.where(row // (2 * per_row) == slot, lengths[slot], position)
        position = position + (row // per_row) % 2
        angles = position.astype(F32) * freq[...]
        return jnp.cos(angles), jnp.sin(angles)

    turns = {size: rotation(rp * size, size) for size in set(SIZES) | {1}}
    k_cos, k_sin = turns[1]

    stats = stat_own[...]
    for d in range(1, n):
        copies[d - 1].wait_recv()
        stats = stats + stat_in[d - 1]

    def as_column(row):
        return jnp.sum(
            jnp.where(diagonal, jnp.broadcast_to(row, (N, N)), 0.0), axis=1, keepdims=True
        )

    mean = as_column(stats[0:1]) / D
    variance = as_column(stats[1:2]) / D - mean * mean
    scaled = (rows.astype(F32) - mean) * lax.rsqrt(variance + eps_norm)
    by_request = (scaled * gain[...].astype(F32)[None]).astype(BF16)
    normed[...] = dot_nn(to_slot, by_request).astype(BF16)

    def project(j):
        start, count = chunk_columns(j)
        if j == 0:
            kv_load.wait()
        q_loads[j].wait()

        @pl.loop(0, count // TILE)
        def _(i):
            at = pl.ds(pl.multiple_of(start + i * TILE, TILE), TILE)
            product = dot_nn(normed[...], wq[:, at])
            for g in range(n):
                partial[g // (2 * H), (g // H) % 2, g % H, :, at] = product[
                    g * rp : (g + 1) * rp
                ]

        at = pl.ds(start, count)
        return send(
            partial.at[1 - core, :, :, :, at],
            from_core.at[:, :, :, at],
            core_send.at[j],
            core_recv.at[j],
            sibling,
        )

    def add_core(j, copy):
        start, count = chunk_columns(j)
        at = pl.ds(start, count)
        copy.wait_recv()
        from_core[1 - mid, :, :, at] = from_core[1 - mid, :, :, at] + partial[core, 1 - mid, :, :, at]
        copy = send(
            from_core.at[1 - mid, :, :, at],
            from_mid.at[:, :, at],
            mid_send.at[j],
            mid_recv.at[j],
            across,
        )
        from_core[mid, :, :, at] = from_core[mid, :, :, at] + partial[core, mid, :, :, at]
        return copy

    def add_mid(j, copy):
        start, count = chunk_columns(j)
        at = pl.ds(start, count)
        copy.wait_recv()
        from_mid[:, :, at] = from_mid[:, :, at] + from_core[mid, :, :, at]
        return [
            send(
                from_mid.at[ahead[d], :, at],
                from_hi.at[d - 1, :, at],
                hi_send.at[j, d - 1],
                hi_recv.at[j, d - 1],
                index_of(ahead[d], mid, core),
            )
            for d in range(1, H)
        ]

    def turn(lower, upper, cosines, sines):
        return jnp.concatenate(
            [lower * cosines - upper * sines, upper * cosines + lower * sines], axis=1
        )

    def attend(j, copies):
        start, count = chunk_columns(j)
        size = SIZES[j]
        q_cos, q_sin = turns[size]
        at = pl.ds(start, count)
        for copy in copies:
            copy.wait_recv()
        rows = from_mid[hi, :, at]
        for d in range(1, H):
            rows = rows + from_hi[d - 1, :, at]
        q_start = 0
        if j == 0:
            q_start = KV
            keys = turn(rows[:, :HALF], rows[:, HALF:HD], k_cos, k_sin)
            both = jnp.concatenate([keys, rows[:, HD:KV]], axis=1)
            at_row = lax.broadcasted_iota(jnp.int32, (128, KV), 0)
            for slot in range(slots):
                one = jnp.broadcast_to(both[2 * slot : 2 * slot + 1], (128, KV))
                two = jnp.broadcast_to(both[2 * slot + 1 : 2 * slot + 2], (128, KV))
                padded = jnp.where(at_row == 0, one, jnp.where(at_row == 1, two, 0.0))
                new_kv[slot] = padded.astype(BF16)
            cache_load.wait()
        for h in range(size):
            for part in range(2):
                begin = q_start + h * HD + part * HALF
                query[part, pl.ds(h, rp, stride=size), :] = rows[:, begin : begin + HALF]
        queries = turn(query[0, : rp * size], query[1, : rp * size], q_cos, q_sin)
        scale = HD ** (-0.5)
        context = cache.shape[1]
        span = 2 * size
        lane_old = lax.broadcasted_iota(jnp.int32, (span, context), 1)
        lane_new = lax.broadcasted_iota(jnp.int32, (span, 128), 1)
        step = lax.broadcasted_iota(jnp.int32, (span, 128), 0) // size
        results = []
        for slot in range(slots):
            q = queries[slot * span : (slot + 1) * span].astype(BF16)
            old = dot_nt(q, cache[slot, :, :HD]) * scale
            new = dot_nt(q, new_kv[slot, :, :HD]) * scale
            old = jnp.where(lane_old < lengths[slot], old, -jnp.inf)
            new = jnp.where(lane_new <= step, new, -jnp.inf)
            peak = jnp.maximum(
                jnp.max(old, axis=1, keepdims=True), jnp.max(new, axis=1, keepdims=True)
            )
            old = jnp.exp(old - peak)
            new = jnp.exp(new - peak)
            denominator = jnp.sum(old, axis=1, keepdims=True) + jnp.sum(
                new, axis=1, keepdims=True
            )
            weighted = dot_nn(old.astype(BF16), cache[slot, :, HD:])
            weighted = weighted + dot_nn(new.astype(BF16), new_kv[slot, :, HD:])
            results.append(weighted / denominator)
        gathered[j][core, mid, hi] = jnp.concatenate(results, axis=0).astype(BF16)
        block = gathered[j].at[core, mid, hi]
        return [
            send(
                block,
                block,
                ghi_send.at[j, d - 1],
                ghi_recv.at[j, d - 1],
                index_of(ahead[d], mid, core),
            )
            for d in range(1, H)
        ]

    def pass_mid(j, copies):
        for copy in copies:
            copy.wait_recv()
        block = gathered[j].at[core, mid]
        return send(block, block, gmid_send.at[j], gmid_recv.at[j], across)

    def pass_core(j, copy):
        copy.wait_recv()
        block = gathered[j].at[core]
        return send(block, block, gcore_send.at[j], gcore_recv.at[j], sibling)

    def mix(j, copy):
        copy.wait_recv()
        o_loads[j].wait()
        size = SIZES[j]
        width = size * HD
        first_row = STARTS[j] * HD
        everything = gathered[j][...].reshape(N * size, HD).astype(F32)
        spread[0, : N * size] = everything[:, :HALF]
        spread[1, : N * size] = everything[:, HALF:]
        for h in range(size):
            head = jnp.concatenate(
                [spread[part, pl.ds(h, N, stride=size), :] for part in range(2)], axis=1
            ).astype(BF16)
            lhs[:, h * HD : (h + 1) * HD] = dot_nn(to_request, head).astype(BF16)

        for k in range(0, width, 512):
            product = dot_nn(lhs[:, k : k + 512], wo[first_row + k : first_row + k + 512, :])
            if j == 0 and k == 0:
                total[...] = product
            else:
                total[...] += product

    held = [None] * GROUPS
    steps = (project, add_core, add_mid, attend, pass_mid, pass_core, mix)
    later = q_loads[2:] + [cache_load] + o_loads
    for stage, j in SCHEDULE:
        for copy in later[:LOADS_A_STEP]:
            copy.start()
        later = later[LOADS_A_STEP:]
        held[j] = project(j) if stage == 0 else steps[stage](j, held[j])
    for copy in sent:
        copy.wait_send()


def on_device(
    n, first_tokens, second_tokens, ln_gain, qkv_weight, out_weight, kv_cache, lengths, order
):
    R, features = first_tokens.shape
    slots, context, _ = kv_cache.shape
    N, rp, H = 2 * R, 2 * slots, n // 4
    columns = qkv_weight.shape[1]
    frequencies = (10000.0 ** (-np.arange(HALF) / HALF)).astype(np.float32)[None]
    anywhere = pl.BlockSpec(memory_space=pl.ANY)
    vmem = pl.BlockSpec(memory_space=pltpu.VMEM)
    dma = pltpu.SemaphoreType.DMA
    mixed = pl.pallas_call(
        functools.partial(kernel, n, slots),
        out_shape=jax.ShapeDtypeStruct((N, features), F32),
        in_specs=[anywhere] * 9,
        out_specs=vmem,
        scratch_shapes=[
            pltpu.VMEM((N, features), BF16),
            pltpu.VMEM((features,), BF16),
            pltpu.VMEM((1, HALF), F32),
            pltpu.SMEM((slots,), jnp.int32),
            pltpu.SMEM((R,), jnp.int32),
            pltpu.VMEM((features, columns), BF16),
            pltpu.VMEM((HEADS * HD, features), BF16),
            pltpu.VMEM((slots, context, KV), BF16),
            pltpu.VMEM((2, N), F32),
            pltpu.VMEM((n - 1, 2, N), F32),
            pltpu.VMEM((N, features), BF16),
            pltpu.VMEM((2, 2, H, rp, columns), F32),
            pltpu.VMEM((2, H, rp, columns), F32),
            pltpu.VMEM((H, rp, columns), F32),
            pltpu.VMEM((H - 1, rp, columns), F32),
            pltpu.VMEM((2, rp * max(SIZES), HALF), F32),
            pltpu.VMEM((slots, 128, KV), BF16),
            tuple(pltpu.VMEM((2, 2, H, rp * size, HD), BF16) for size in SIZES),
            pltpu.VMEM((2, N * max(SIZES), HALF), F32),
            pltpu.VMEM((N, max(SIZES) * HD), BF16),
            dma((7,)),
            dma((GROUPS + 1,)),
            dma((GROUPS,)),
            dma((n - 1,)),
            dma((n - 1,)),
            dma((GROUPS,)),
            dma((GROUPS,)),
            dma((GROUPS,)),
            dma((GROUPS,)),
            dma((GROUPS, H - 1)),
            dma((GROUPS, H - 1)),
            dma((GROUPS, H - 1)),
            dma((GROUPS, H - 1)),
            dma((GROUPS,)),
            dma((GROUPS,)),
            dma((GROUPS,)),
            dma((GROUPS,)),
        ],
        compiler_params=pltpu.CompilerParams(
            collective_id=0, has_side_effects=True, vmem_limit_bytes=56 * 2**20
        ),
    )(
        first_tokens,
        second_tokens,
        ln_gain,
        jnp.asarray(frequencies),
        qkv_weight,
        out_weight,
        kv_cache,
        lengths,
        order,
    )
    first_out = (first_tokens.astype(F32) + mixed[:R]).astype(BF16)
    second_out = (second_tokens.astype(F32) + mixed[R:]).astype(BF16)
    return first_out, second_out


def solution(mesh):
    return jax.shard_map(
        functools.partial(on_device, mesh.shape["gx"]),
        mesh=mesh,
        in_specs=(
            P("rep", "gx"),
            P("rep", "gx"),
            P("gx"),
            P("gx", None),
            P(None, "gx"),
            P(("rep", "gx"), None, None),
            P(("rep", "gx")),
            P("rep"),
        ),
        out_specs=(P("rep", "gx"), P("rep", "gx")),
        check_vma=False,
    )
```

```python
import functools

import jax
import jax.numpy as jnp
import numpy as np
from jax import lax
from jax.experimental import pallas as pl
from jax.experimental.pallas import tpu as pltpu
from jax.sharding import PartitionSpec as P

D = 18432
HEADS = 24
HD = 256
HALF = HD // 2
KV = 2 * HD

SIZES = (8, 8, 8)
STARTS = (0, 8, 16)
GROUPS = len(SIZES)
TILE = 512
LOADS_A_STEP = 1

SCHEDULE = (
    (0, 0), (0, 1), (1, 0), (0, 2), (1, 1), (0, 3), (1, 2), (0, 4), (2, 0), (1, 3), (1, 4),
    (2, 1), (2, 2), (3, 0), (2, 3), (2, 4), (3, 1), (4, 0), (3, 2), (4, 1), (5, 0), (4, 2),
    (5, 1), (6, 0), (6, 1), (6, 2),
)

eps_norm = 1e-05

F32 = jnp.float32
BF16 = jnp.bfloat16


def dot_nt(a, b):
    return lax.dot_general(a, b, (((1,), (1,)), ((), ())), preferred_element_type=F32)


def dot_nn(a, b):
    return jnp.dot(a, b, preferred_element_type=F32)


PIECES = (
    (0, 1536, 0),
    (1536, 1024, 0),
    (2560, 2048, 1),
    (4608, 1024, 2),
    (5632, 1024, 2),
)


def kernel(
    n,
    slots,
    first_ref,
    second_ref,
    gain_ref,
    freq_ref,
    qkv_ref,
    out_w_ref,
    cache_ref,
    lengths_ref,
    order_ref,
    total,
    x,
    gain,
    freq,
    lengths,
    order,
    wq,
    wo,
    cache,
    stat_own,
    stat_in,
    normed,
    partial,
    from_core,
    from_mid,
    from_hi,
    query,
    new_kv,
    gathered,
    spread,
    lhs,
    in_sem,
    q_sem,
    o_sem,
    stat_send,
    stat_recv,
    core_send,
    core_recv,
    mid_send,
    mid_recv,
    hi_send,
    hi_recv,
    ghi_send,
    ghi_recv,
    gmid_send,
    gmid_recv,
    gcore_send,
    gcore_recv,
    row_send,
    row_recv,
):
    H = n // 4
    R = order_ref.shape[0]
    N = 2 * R
    rp = 2 * slots
    me = lax.axis_index("gx")
    core, mid, hi = me % 2, (me // 2) % 2, me // 4

    def index_of(hi_at, mid_at, core_at):
        return (hi_at * 2 + mid_at) * 2 + core_at

    sibling = index_of(hi, mid, 1 - core)
    across = index_of(hi, 1 - mid, core)
    ahead = [lax.rem(hi + d, H) for d in range(H)]
    behind = [lax.rem(hi - d + H, H) for d in range(H)]

    barrier = pltpu.get_barrier_semaphore()
    partners = [lax.rem(me + d, n) for d in range(1, n)]
    for partner in partners:
        pl.semaphore_signal(
            barrier, inc=1, device_id={"gx": partner}, device_id_type=pl.DeviceIdType.MESH
        )

    loads = [
        pltpu.make_async_copy(src, dst, in_sem.at[i])
        for i, (src, dst) in enumerate(
            [
                (first_ref, x.at[pl.ds(0, R)]),
                (second_ref, x.at[pl.ds(R, R)]),
                (gain_ref, gain),
                (freq_ref, freq),
                (lengths_ref, lengths),
                (order_ref, order),
            ]
        )
    ]
    kv_load = pltpu.make_async_copy(
        qkv_ref.at[:, pl.ds(HEADS * HD, KV)], wq.at[:, pl.ds(0, KV)], q_sem.at[GROUPS]
    )
    q_loads = [
        pltpu.make_async_copy(
            qkv_ref.at[:, pl.ds(start * HD, size * HD)],
            wq.at[:, pl.ds(KV + start * HD, size * HD)],
            q_sem.at[j],
        )
        for j, (start, size) in enumerate(zip(STARTS, SIZES))
    ]
    cache_load = pltpu.make_async_copy(cache_ref, cache, in_sem.at[6])
    o_loads = [
        pltpu.make_async_copy(
            out_w_ref.at[pl.ds(start * HD, size * HD)],
            wo.at[pl.ds(start * HD, size * HD)],
            o_sem.at[j],
        )
        for j, (start, size) in enumerate(zip(STARTS, SIZES))
    ]
    for copy in loads + [kv_load, q_loads[0]]:
        copy.start()

    sent = []

    def send(src, dst, send_sem, recv_sem, partner):
        copy = pltpu.make_async_remote_copy(
            src_ref=src,
            dst_ref=dst,
            send_sem=send_sem,
            recv_sem=recv_sem,
            device_id={"gx": partner},
            device_id_type=pl.DeviceIdType.MESH,
        )
        copy.start()
        sent.append(copy)
        return copy

    for copy in loads:
        copy.wait()
    rows = x[...]
    features = rows.shape[1]
    square = lax.broadcasted_iota(jnp.int32, (N, N), 0)
    across_lanes = lax.broadcasted_iota(jnp.int32, (N, N), 1)
    diagonal = square == across_lanes
    sums = dot_nt(jnp.ones((8, features), BF16), rows)
    squares = jnp.sum(jnp.where(diagonal, dot_nt(rows, rows), 0.0), axis=0, keepdims=True)
    line = lax.broadcasted_iota(jnp.int32, (8, N), 0)
    stat_own[...] = jnp.where(line == 0, sums, jnp.broadcast_to(squares, (8, N)))[:2]

    pl.semaphore_wait(barrier, n - 1)
    copies = [
        send(stat_own, stat_in.at[d - 1], stat_send.at[d - 1], stat_recv.at[d - 1], partners[d - 1])
        for d in range(1, n)
    ]
    for copy in [q_loads[1]]:
        copy.start()

    lane = lax.broadcasted_iota(jnp.int32, (8, N), 1)
    holder = jnp.zeros((8, N), jnp.int32)
    for p in range(R):
        device, slot = p // slots, p % slots
        at = (((device % 2) * 2 + (device // 2) % 2) * H + device // 4) * slots + slot
        holder = jnp.where(lane // 2 == at, order[p], holder)
    holder = holder + (lane % 2) * R
    to_request = jnp.where(square == jnp.broadcast_to(holder[:1], (N, N)), 1.0, 0.0).astype(BF16)
    unit = jnp.where(diagonal, 1.0, 0.0).astype(BF16)
    to_slot = dot_nt(unit, to_request).astype(BF16)

    def rotation(count, per_row):
        row = lax.broadcasted_iota(jnp.int32, (count, HALF), 0)
        position = jnp.zeros((count, HALF), jnp.int32)
        for slot in range(slots):
            position = jnp.where(row // (2 * per_row) == slot, lengths[slot], position)
        position = position + (row // per_row) % 2
        angles = position.astype(F32) * freq[...]
        return jnp.cos(angles), jnp.sin(angles)

    turns = {size: rotation(rp * size, size) for size in set(SIZES) | {1}}
    k_cos, k_sin = turns[1]

    stats = stat_own[...]
    for d in range(1, n):
        copies[d - 1].wait_recv()
        stats = stats + stat_in[d - 1]

    def as_column(row):
        return jnp.sum(
            jnp.where(diagonal, jnp.broadcast_to(row, (N, N)), 0.0), axis=1, keepdims=True
        )

    mean = as_column(stats[0:1]) / D
    variance = as_column(stats[1:2]) / D - mean * mean
    scaled = (rows.astype(F32) - mean) * lax.rsqrt(variance + eps_norm)
    by_request = (scaled * gain[...].astype(F32)[None]).astype(BF16)
    normed[...] = dot_nn(to_slot, by_request).astype(BF16)

    def project(j):
        start, count, group = PIECES[j]
        if j == 0:
            kv_load.wait()
        if j == 0 or PIECES[j - 1][2] != group:
            q_loads[group].wait()

        @pl.loop(0, count // TILE)
        def _(i):
            at = pl.ds(pl.multiple_of(start + i * TILE, TILE), TILE)
            product = dot_nn(normed[...], wq[:, at])
            for g in range(n):
                partial[g // (2 * H), (g // H) % 2, g % H, :, at] = product[
                    g * rp : (g + 1) * rp
                ]

        at = pl.ds(start, count)
        return send(
            partial.at[1 - core, :, :, :, at],
            from_core.at[:, :, :, at],
            core_send.at[j],
            core_recv.at[j],
            sibling,
        )

    def add_core(j, copy):
        start, count, _ = PIECES[j]
        at = pl.ds(start, count)
        copy.wait_recv()
        from_core[1 - mid, :, :, at] = from_core[1 - mid, :, :, at] + partial[core, 1 - mid, :, :, at]
        copy = send(
            from_core.at[1 - mid, :, :, at],
            from_mid.at[:, :, at],
            mid_send.at[j],
            mid_recv.at[j],
            across,
        )
        from_core[mid, :, :, at] = from_core[mid, :, :, at] + partial[core, mid, :, :, at]
        return copy

    def add_mid(j, copy):
        start, count, _ = PIECES[j]
        at = pl.ds(start, count)
        copy.wait_recv()
        from_mid[:, :, at] = from_mid[:, :, at] + from_core[mid, :, :, at]
        return [
            send(
                from_mid.at[ahead[d], :, at],
                from_hi.at[d - 1, :, at],
                hi_send.at[j, d - 1],
                hi_recv.at[j, d - 1],
                index_of(ahead[d], mid, core),
            )
            for d in range(1, H)
        ]

    def turn(lower, upper, cosines, sines):
        return jnp.concatenate(
            [lower * cosines - upper * sines, upper * cosines + lower * sines], axis=1
        )

    def attend(j, copies):
        start = min(first for first, _, group in PIECES if group == j)
        count = sum(columns for _, columns, group in PIECES if group == j)
        size = SIZES[j]
        q_cos, q_sin = turns[size]
        at = pl.ds(start, count)
        for copy in copies:
            copy.wait_recv()
        rows = from_mid[hi, :, at]
        for d in range(1, H):
            rows = rows + from_hi[d - 1, :, at]
        q_start = 0
        if j == 0:
            q_start = KV
            keys = turn(rows[:, :HALF], rows[:, HALF:HD], k_cos, k_sin)
            both = jnp.concatenate([keys, rows[:, HD:KV]], axis=1)
            at_row = lax.broadcasted_iota(jnp.int32, (128, KV), 0)
            for slot in range(slots):
                one = jnp.broadcast_to(both[2 * slot : 2 * slot + 1], (128, KV))
                two = jnp.broadcast_to(both[2 * slot + 1 : 2 * slot + 2], (128, KV))
                padded = jnp.where(at_row == 0, one, jnp.where(at_row == 1, two, 0.0))
                new_kv[slot] = padded.astype(BF16)
            cache_load.wait()
        for h in range(size):
            for part in range(2):
                begin = q_start + h * HD + part * HALF
                query[part, pl.ds(h, rp, stride=size), :] = rows[:, begin : begin + HALF]
        queries = turn(query[0, : rp * size], query[1, : rp * size], q_cos, q_sin)
        scale = HD ** (-0.5)
        context = cache.shape[1]
        span = 2 * size
        lane_old = lax.broadcasted_iota(jnp.int32, (span, context), 1)
        lane_new = lax.broadcasted_iota(jnp.int32, (span, 128), 1)
        step = lax.broadcasted_iota(jnp.int32, (span, 128), 0) // size
        results = []
        for slot in range(slots):
            q = queries[slot * span : (slot + 1) * span].astype(BF16)
            old = dot_nt(q, cache[slot, :, :HD]) * scale
            new = dot_nt(q, new_kv[slot, :, :HD]) * scale
            old = jnp.where(lane_old < lengths[slot], old, -jnp.inf)
            new = jnp.where(lane_new <= step, new, -jnp.inf)
            peak = jnp.maximum(
                jnp.max(old, axis=1, keepdims=True), jnp.max(new, axis=1, keepdims=True)
            )
            old = jnp.exp(old - peak)
            new = jnp.exp(new - peak)
            denominator = jnp.sum(old, axis=1, keepdims=True) + jnp.sum(
                new, axis=1, keepdims=True
            )
            weighted = dot_nn(old.astype(BF16), cache[slot, :, HD:])
            weighted = weighted + dot_nn(new.astype(BF16), new_kv[slot, :, HD:])
            results.append(weighted / denominator)
        gathered[j][core, mid, hi] = jnp.concatenate(results, axis=0).astype(BF16)
        block = gathered[j].at[core, mid, hi]
        return [
            send(
                block,
                block,
                ghi_send.at[j, d - 1],
                ghi_recv.at[j, d - 1],
                index_of(ahead[d], mid, core),
            )
            for d in range(1, H)
        ]

    def pass_mid(j, copies):
        for copy in copies:
            copy.wait_recv()
        block = gathered[j].at[core, mid]
        copy = send(block, block, gmid_send.at[j], gmid_recv.at[j], across)
        if j < GROUPS - 1:
            return copy
        others = [index_of(hi, mid, 1 - core), index_of(hi, 1 - mid, 1 - core)]
        return [copy] + [
            send(block, block, row_send.at[k], row_recv.at[k], partner)
            for k, partner in enumerate(others)
        ]

    def pass_core(j, copy):
        copy.wait_recv()
        block = gathered[j].at[core]
        return send(block, block, gcore_send.at[j], gcore_recv.at[j], sibling)

    def mix(j, copies):
        for copy in copies if j == GROUPS - 1 else [copies]:
            copy.wait_recv()
        o_loads[j].wait()
        size = SIZES[j]
        width = size * HD
        first_row = STARTS[j] * HD
        everything = gathered[j][...].reshape(N * size, HD).astype(F32)
        spread[0, : N * size] = everything[:, :HALF]
        spread[1, : N * size] = everything[:, HALF:]
        for h in range(size):
            head = jnp.concatenate(
                [spread[part, pl.ds(h, N, stride=size), :] for part in range(2)], axis=1
            ).astype(BF16)
            lhs[:, h * HD : (h + 1) * HD] = dot_nn(to_request, head).astype(BF16)

        for k in range(0, width, 512):
            product = dot_nn(lhs[:, k : k + 512], wo[first_row + k : first_row + k + 512, :])
            if j == 0 and k == 0:
                total[...] = product
            else:
                total[...] += product

    held = [None] * GROUPS
    summed = [None] * len(PIECES)
    steps = (project, add_core, add_mid, attend, pass_mid, pass_core, mix)
    later = q_loads[2:] + [cache_load] + o_loads
    for stage, j in SCHEDULE:
        for copy in later[:LOADS_A_STEP]:
            copy.start()
        later = later[LOADS_A_STEP:]
        if stage == 0:
            summed[j] = project(j)
        elif stage < 3:
            summed[j] = steps[stage](j, summed[j])
        elif stage == 3:
            pieces = [copies for copies, piece in zip(summed, PIECES) if piece[2] == j]
            held[j] = attend(j, [copy for copies in pieces for copy in copies])
        else:
            held[j] = steps[stage](j, held[j])
    for copy in sent:
        copy.wait_send()


def on_device(
    n, first_tokens, second_tokens, ln_gain, qkv_weight, out_weight, kv_cache, lengths, order
):
    R, features = first_tokens.shape
    slots, context, _ = kv_cache.shape
    N, rp, H = 2 * R, 2 * slots, n // 4
    columns = qkv_weight.shape[1]
    frequencies = (10000.0 ** (-np.arange(HALF) / HALF)).astype(np.float32)[None]
    anywhere = pl.BlockSpec(memory_space=pl.ANY)
    vmem = pl.BlockSpec(memory_space=pltpu.VMEM)
    dma = pltpu.SemaphoreType.DMA
    mixed = pl.pallas_call(
        functools.partial(kernel, n, slots),
        out_shape=jax.ShapeDtypeStruct((N, features), F32),
        in_specs=[anywhere] * 9,
        out_specs=vmem,
        scratch_shapes=[
            pltpu.VMEM((N, features), BF16),
            pltpu.VMEM((features,), BF16),
            pltpu.VMEM((1, HALF), F32),
            pltpu.SMEM((slots,), jnp.int32),
            pltpu.SMEM((R,), jnp.int32),
            pltpu.VMEM((features, columns), BF16),
            pltpu.VMEM((HEADS * HD, features), BF16),
            pltpu.VMEM((slots, context, KV), BF16),
            pltpu.VMEM((2, N), F32),
            pltpu.VMEM((n - 1, 2, N), F32),
            pltpu.VMEM((N, features), BF16),
            pltpu.VMEM((2, 2, H, rp, columns), F32),
            pltpu.VMEM((2, H, rp, columns), F32),
            pltpu.VMEM((H, rp, columns), F32),
            pltpu.VMEM((H - 1, rp, columns), F32),
            pltpu.VMEM((2, rp * max(SIZES), HALF), F32),
            pltpu.VMEM((slots, 128, KV), BF16),
            tuple(pltpu.VMEM((2, 2, H, rp * size, HD), BF16) for size in SIZES),
            pltpu.VMEM((2, N * max(SIZES), HALF), F32),
            pltpu.VMEM((N, max(SIZES) * HD), BF16),
            dma((7,)),
            dma((GROUPS + 1,)),
            dma((GROUPS,)),
            dma((n - 1,)),
            dma((n - 1,)),
            dma((len(PIECES),)),
            dma((len(PIECES),)),
            dma((len(PIECES),)),
            dma((len(PIECES),)),
            dma((len(PIECES), H - 1)),
            dma((len(PIECES), H - 1)),
            dma((GROUPS, H - 1)),
            dma((GROUPS, H - 1)),
            dma((GROUPS,)),
            dma((GROUPS,)),
            dma((GROUPS,)),
            dma((GROUPS,)),
            dma((2,)),
            dma((2,)),
        ],
        compiler_params=pltpu.CompilerParams(
            collective_id=0, has_side_effects=True, vmem_limit_bytes=56 * 2**20
        ),
    )(
        first_tokens,
        second_tokens,
        ln_gain,
        jnp.asarray(frequencies),
        qkv_weight,
        out_weight,
        kv_cache,
        lengths,
        order,
    )
    first_out = (first_tokens.astype(F32) + mixed[:R]).astype(BF16)
    second_out = (second_tokens.astype(F32) + mixed[R:]).astype(BF16)
    return first_out, second_out


def solution(mesh):
    return jax.shard_map(
        functools.partial(on_device, mesh.shape["gx"]),
        mesh=mesh,
        in_specs=(
            P("rep", "gx"),
            P("rep", "gx"),
            P("gx"),
            P("gx", None),
            P(None, "gx"),
            P(("rep", "gx"), None, None),
            P(("rep", "gx")),
            P("rep"),
        ),
        out_specs=(P("rep", "gx"), P("rep", "gx")),
        check_vma=False,
    )
```
